128 devices in a mesh: dp: 8 (over z, core), tensor: 16 (over y, x).
Axes of the slice: x: 4, y: 4, z: 4, core: 2. Of those that a mesh axis runs over, the one named last changes fastest.
Arguments:
- kept_block_input: bfloat16 [8, 128, 16384], P('dp', 'tensor'), may hold values from -6 to 6
- block_output_gradient: bfloat16 [8, 128, 16384], P('dp', 'tensor'), may hold values from -6 to 6
- gate_preact_kept: bfloat16 [8, 128, 26624], P('dp', None, 'tensor'), may hold values from -8 to 8
- up_preact_kept: bfloat16 [8, 128, 26624], P('dp', None, 'tensor'), may hold values from -6 to 6
- gate_weight: bfloat16 [16384, 26624], P('dp', 'tensor'), may hold values from -0.046875 to 0.046875
- up_weight: bfloat16 [16384, 26624], P('dp', 'tensor'), may hold values from -0.046875 to 0.046875
- down_weight: bfloat16 [26624, 16384], P('tensor', 'dp'), may hold values from -0.0390625 to 0.0390625
- adapter_down_maps: bfloat16 [2, 16, 16384], replicated, may hold values from -0.046875 to 0.046875
- adapter_up_maps: bfloat16 [2, 16, 26624], P(None, None, 'tensor'), may hold values from -0.0390625 to 0.0390625
Outputs:
- block_input_gradient: bfloat16 [8, 128, 16384], P('dp', 'tensor')
- adapter_down_gradient: float32 [2, 16, 16384], replicated
- adapter_up_gradient: float32 [2, 16, 26624], P(None, None, 'tensor')
The draws below stay inside these ranges and needn't reach their ends.
All inputs are finite; a program needn't handle non-finite values.
Results may differ from the reference program's by a relative error of at most 0.019.
Values may be sent and summed in bfloat16 or wider, within the bound.
A program may use at most 128 MiB of HBM per device.

```python
import jax
import jax.numpy as jnp
from jax import lax

MODEL_DIM = 16384
HIDDEN_UNITS = 26624
ADAPTER_RANK = 16
HB = 128
GROUP_TOK = 128
TOKENS = 1024
N_DP = 8


def steps_of(stream_key, dims, split, least, high):
    def one(dim, parts):
        steps = jax.random.uniform(jax.random.fold_in(jax.random.fold_in(stream_key, 6), dim), (parts,), jnp.float32, least / len(split), high / len(split))
        return jnp.repeat(jnp.exp(steps), dims[dim] // parts).reshape((-1,) + (1,) * (len(dims) - dim - 1))

    level = one(*split[0])
    for cut in split[1:]:
        level = level * one(*cut)
    return level


def normal_values(rng, shape, spread, bound, pieces=(), kind=jnp.bfloat16):
    values = spread * jax.random.normal(rng, shape, jnp.float32)
    if pieces:
        values = values * steps_of(rng, shape, pieces, -0.22, 0.18)
    return jnp.clip(values, -bound, bound).astype(kind)


def setup_inputs(seed: int = 0) -> dict:
    keys = jax.random.split(jax.random.key(seed), 10)
    return {
        "kept_block_input": normal_values(keys[0], (N_DP, GROUP_TOK, MODEL_DIM), 1.0, 6.0, ((0, 8), (1, 16))),
        "block_output_gradient": normal_values(keys[1], (N_DP, GROUP_TOK, MODEL_DIM), 1.0, 6.0, ((0, 8), (1, 16))),
        "gate_preact_kept": normal_values(keys[2], (N_DP, GROUP_TOK, HIDDEN_UNITS), 1.5, 8.0, ((0, 8), (2, 16))),
        "up_preact_kept": normal_values(keys[3], (N_DP, GROUP_TOK, HIDDEN_UNITS), 1.0, 6.0, ((0, 8), (2, 16))),
        "gate_weight": normal_values(keys[4], (MODEL_DIM, HIDDEN_UNITS), MODEL_DIM ** -0.5, 0.046875, ((0, 8), (1, 16))),
        "up_weight": normal_values(keys[5], (MODEL_DIM, HIDDEN_UNITS), MODEL_DIM ** -0.5, 0.046875, ((0, 8), (1, 16))),
        "down_weight": normal_values(keys[6], (HIDDEN_UNITS, MODEL_DIM), HIDDEN_UNITS ** -0.5, 0.0390625, ((0, 16), (1, 8))),
        "adapter_down_maps": normal_values(keys[7], (2, ADAPTER_RANK, MODEL_DIM), MODEL_DIM ** -0.5, 0.046875),
        "adapter_up_maps": normal_values(keys[8], (2, ADAPTER_RANK, HIDDEN_UNITS), HIDDEN_UNITS ** -0.5, 0.0390625, ((2, 16),)),
    }


ADAPTER_SCALE = 2.0

def hadamard(length):
    positions = jnp.arange(length, dtype=jnp.int32)
    common_bits = jnp.bitwise_and(positions[:, None], positions[None, :])
    parity = jnp.zeros((length, length), jnp.int32)
    for bit_index in range(length.bit_length() - 1):
        parity = parity + jnp.bitwise_and(jnp.right_shift(common_bits, bit_index), 1)
    signs = (1 - 2 * (parity % 2)).astype(jnp.float32)
    return signs / jnp.sqrt(jnp.float32(length))

def rotate(values):
    table = hadamard(HB)
    array_shape = values.shape
    blocks = values.astype(jnp.float32).reshape(array_shape[:-1] + (array_shape[-1] // HB, HB))
    turned = jnp.einsum('tkb,bc->tkc', blocks.reshape((-1, array_shape[-1] // HB, HB)), table, precision=lax.Precision.HIGHEST)
    return turned.reshape(array_shape).astype(jnp.bfloat16)

def reference(kept_block_input, block_output_gradient, gate_preact_kept, up_preact_kept, gate_weight, up_weight, down_weight, adapter_down_maps, adapter_up_maps):
    token_rows = TOKENS
    inputs = rotate(kept_block_input).reshape(token_rows, MODEL_DIM)
    grads = rotate(block_output_gradient).reshape(token_rows, MODEL_DIM)
    adapter_lookup = adapter_down_maps.reshape(2 * ADAPTER_RANK, MODEL_DIM)
    adown = jnp.dot(inputs, adapter_lookup.T, preferred_element_type=jnp.float32).astype(jnp.bfloat16)
    hidden_grad = jnp.dot(grads, down_weight.T, preferred_element_type=jnp.float32)
    gate_pre = gate_preact_kept.reshape(token_rows, HIDDEN_UNITS).astype(jnp.float32)
    up_pre = up_preact_kept.reshape(token_rows, HIDDEN_UNITS).astype(jnp.float32)
    squash = jax.nn.sigmoid(gate_pre)
    gate_gradient = (hidden_grad * up_pre * squash * (1.0 + gate_pre * (1.0 - squash))).astype(jnp.bfloat16)
    up_gradient = (hidden_grad * gate_pre * squash).astype(jnp.bfloat16)
    gate_rank_value = jnp.dot(gate_gradient, adapter_up_maps[0].T, preferred_element_type=jnp.float32)
    up_rank_value = jnp.dot(up_gradient, adapter_up_maps[1].T, preferred_element_type=jnp.float32)
    rank_partials = jnp.concatenate([gate_rank_value, up_rank_value], axis=1)
    block_input_gradient = jnp.dot(gate_gradient, gate_weight.T, preferred_element_type=jnp.float32)
    block_input_gradient = block_input_gradient + jnp.dot(up_gradient, up_weight.T, preferred_element_type=jnp.float32)
    block_input_gradient = block_input_gradient + ADAPTER_SCALE * jnp.dot(rank_partials, adapter_lookup.astype(jnp.float32), precision=lax.Precision.HIGHEST)
    block_input_gradient = block_input_gradient.astype(jnp.bfloat16).reshape(N_DP, GROUP_TOK, MODEL_DIM)
    gradient_scale = ADAPTER_SCALE / token_rows ** 0.5
    gate_up_map = jnp.dot(adown[:, :ADAPTER_RANK].T, gate_gradient, preferred_element_type=jnp.float32)
    up_branch_map = jnp.dot(adown[:, ADAPTER_RANK:].T, up_gradient, preferred_element_type=jnp.float32)
    adapter_up_gradient = jnp.stack([gate_up_map, up_branch_map]) * gradient_scale
    down_map_terms = jnp.dot(rank_partials.T, inputs.astype(jnp.float32), precision=lax.Precision.HIGHEST)
    adapter_down_gradient = down_map_terms.reshape(2, ADAPTER_RANK, MODEL_DIM) * gradient_scale
    return (block_input_gradient, adapter_down_gradient, adapter_up_gradient)
```

```python
import functools

import jax
import jax.numpy as jnp
import numpy as np
from jax import lax
from jax.experimental import pallas as pl
from jax.experimental.pallas import tpu as pltpu
from jax.sharding import PartitionSpec as P

F32 = jnp.float32
BF16 = jnp.bfloat16
HB = 128
WIDTH = 16384
SLICE = 2048
HALF = 1024
HID = 1664
RANK = 16
SCALE = 2.0
GRAD_SCALE = SCALE / 1024.0**0.5
ORDER1 = (2, 1, 3, 0)
ORDER2 = (0, 3, 1, 2)
TILES1 = ((0, 640), (640, 512), (1152, 512))
TILE2 = 512
NSEM = 264
NT = (((1,), (1,)), ((), ()))


def sign_table():
    index = np.arange(HB)
    common = index[:, None] & index[None, :]
    parity = np.zeros_like(common)
    for bit in range(7):
        parity += (common >> bit) & 1
    return (1 - 2 * (parity % 2)).astype(np.float32)


def kernel(
    x_ref, dy_ref, g_ref, u_ref, am_ref, um_ref, h_ref, wd_hbm, wg_hbm, wu_hbm,
    out_ref, down_ref, up_ref,
    wd, wg, wu, s_buf, r_buf, y_buf, xg, p_buf, q_buf, f_buf, gz_buf, d_buf, ab, o_buf,
    r1, r2, r3, r4, t_buf, v_buf, ad_s, ad_r, adn, zs, zr, ds_buf, dr_buf, e_buf, a_own, u_pad,
    ss, rs, ws,
):
    d = lax.axis_index("dp")
    t = lax.axis_index("tensor")
    z, c = d // 2, d % 2
    oc = 1 - c
    pos = {"y": t // 4, "x": t % 4}
    count = [0]
    pending = []

    def unit(k):
        return (z + k) % 4

    zp, zm = unit(1), unit(3)
    sib = (z * 2 + oc, t)
    up_dev, down_dev = (zp * 2 + c, t), (zm * 2 + c, t)

    def near(axis, k):
        moved = dict(pos)
        moved[axis] = (pos[axis] + k) % 4
        return (d, moved["y"] * 4 + moved["x"])

    def send(src, dst, dev):
        k = count[0]
        count[0] += 1
        copy = pltpu.make_async_remote_copy(
            src_ref=src, dst_ref=dst, send_sem=ss.at[k], recv_sem=rs.at[k],
            device_id=dev, device_id_type=pl.DeviceIdType.MESH,
        )
        copy.start()
        pending.append(copy)
        return k, copy

    def arrived(k, dst):
        pltpu.make_async_remote_copy(
            src_ref=dst, dst_ref=dst, send_sem=ss.at[k], recv_sem=rs.at[k],
            device_id=sib, device_id_type=pl.DeviceIdType.MESH,
        ).wait_recv()

    def sent(copy):
        copy.wait_send()
        pending[:] = [other for other in pending if other is not copy]

    loads = []
    for k, (src, dst) in enumerate(((wd_hbm, wd), (wg_hbm, wg), (wu_hbm, wu))):
        copy = pltpu.make_async_copy(src, dst, ws.at[k])
        copy.start()
        loads.append(copy)

    barrier = pltpu.get_barrier_semaphore()
    for i in range(1, 8):
        pl.semaphore_signal(barrier, inc=1, device_id=((d + i) % 8, t), device_id_type=pl.DeviceIdType.MESH)
    for i in range(1, 16):
        pl.semaphore_signal(barrier, inc=1, device_id=(d, (t + i) % 16), device_id_type=pl.DeviceIdType.MESH)

    def rotate(src, slot):
        flat = src[0].astype(F32)
        rows = jnp.concatenate([flat[:, HB * k : HB * (k + 1)] for k in range(WIDTH // HB)], axis=0)
        turned = jnp.dot(rows.astype(BF16), h_ref[...], preferred_element_type=F32) * (1.0 / HB**0.5)
        for p in range(8):
            for j in range(8):
                first, second = 8 * (16 * p + j), 8 * (16 * p + 8 + j)
                s_buf[slot, p, :, HB * j : HB * (j + 1)] = jnp.concatenate(
                    [turned[first : first + 8], turned[second : second + 8]], axis=0
                ).astype(BF16)

    rels = [(k, o) for k in (2, 1, 3, 0) for o in (0, 1) if (k, o) != (0, 0)]

    def peer(k, o):
        return unit(k) * 2 + (oc if o else c)

    def source(k, o):
        return unit((4 - k) % 4) * 2 + (oc if o else c)

    rotate(dy_ref, 0)
    pl.semaphore_wait(barrier, 22)
    first_a2a = {}
    for slot in range(2):
        if slot == 1:
            rotate(x_ref, 1)
        for k, o in rels:
            first_a2a[slot, k, o] = send(
                s_buf.at[slot, peer(k, o)], r_buf.at[slot, d], (peer(k, o), t)
            )[0]
        r_buf[slot, d] = s_buf[slot, d]

    def factors(i, carry):
        rows = pl.ds(pl.multiple_of(i * 16, 16), 16)
        gate = g_ref[0, rows, :].astype(F32)
        up = u_ref[0, rows, :].astype(F32)
        squash = 1.0 / (1.0 + jnp.exp(-gate))
        ab[z, 0, c, rows, :] = (up * squash * (1.0 + gate * (1.0 - squash))).astype(BF16)
        ab[z, 1, c, rows, :] = (gate * squash).astype(BF16)
        return carry

    lax.fori_loop(0, 8, factors, 0)

    class ZGather:
        def __init__(self, whole, half):
            self.whole, self.half = whole, half
            self.copies = {0: [], 1: [], 2: [], 3: []}
            self.k_from = {}

        def begin(self):
            self.k_up = self.push(0, self.whole(z, c), up_dev)
            self.k_down = self.push(0, self.whole(z, c), down_dev)
            self.k_from[0] = self.push(0, self.whole(z, c), sib)

        def push(self, owner, ref, dev):
            k, copy = send(ref, ref, dev)
            self.copies[owner].append(copy)
            return k

        def onward(self):
            arrived(self.k_up, self.whole(zm, c))
            self.k_f0 = self.push(3, self.half(zm, c, 0), up_dev)
            self.k_from[3] = self.push(3, self.whole(zm, c), sib)
            arrived(self.k_down, self.whole(zp, c))
            self.k_f1 = self.push(1, self.half(zp, c, 1), down_dev)
            self.k_from[1] = self.push(1, self.whole(zp, c), sib)

        def last(self):
            arrived(self.k_f0, self.half(unit(2), c, 0))
            arrived(self.k_f1, self.half(unit(2), c, 1))
            self.k_from[2] = self.push(2, self.whole(unit(2), c), sib)

        def have(self, rel):
            arrived(self.k_from[rel], self.whole(unit(rel), oc))

        def release(self, rel):
            for copy in self.copies[rel]:
                sent(copy)

    ab_gather = ZGather(
        lambda u, core: ab.at[u, :, core],
        lambda u, core, i: ab.at[u, i, core],
    )
    ab_gather.begin()

    def unpack(slot, u):
        low = r_buf[slot, 2 * u].astype(F32)
        high = r_buf[slot, 2 * u + 1].astype(F32)
        left = jnp.concatenate([low[:8], high[:8]], axis=0).astype(BF16)
        right = jnp.concatenate([low[8:], high[8:]], axis=0).astype(BF16)
        return left, right

    for k, o in rels:
        arrived(first_a2a[0, k, o], r_buf.at[0, source(k, o)])
    for i, rel in enumerate(ORDER1):
        left, right = unpack(0, unit(rel))
        y_buf[i, pos["y"], pos["x"], :, :HALF] = left
        y_buf[i, pos["y"], pos["x"], :, HALF:] = right

    AXES = (("x", "y"), ("y", "x"))

    def block(buf, lead, h, f, g, cols):
        yy, xx = (g, f) if AXES[h][0] == "x" else (f, g)
        return buf.at[lead, yy, xx, :, cols]

    COLS = (pl.ds(0, HALF), pl.ds(HALF, HALF))
    chunks = ((0, 2), (2, 2))
    keys = {}

    def shift(axis, k):
        return (pos[axis] + k) % 4

    def lead_of(n, part):
        start, size = chunks[n]
        if part == "all":
            return pl.ds(start, size)
        return pl.ds(start, size // 2) if part == "first" else pl.ds(start + size // 2, size // 2)

    def ag1_ref(n, h, fr, part):
        f_axis, g_axis = AXES[h]
        return block(y_buf, lead_of(n, part), h, shift(f_axis, fr), pos[g_axis], COLS[h])

    def ag2_ref(n, h, fr, gr, part):
        f_axis, g_axis = AXES[h]
        return block(y_buf, lead_of(n, part), h, shift(f_axis, fr), shift(g_axis, gr), COLS[h])

    def ag_push(key, ref, axis, k):
        keys[key] = send(ref, ref, near(axis, k))[0]

    def stage2_own(n, h, fr):
        g_axis = AXES[h][1]
        for k in (1, -1):
            ag_push(("2", n, h, fr, k), ag2_ref(n, h, fr, 0, "all"), g_axis, k)

    def stage2_onward(n, h, fr):
        g_axis = AXES[h][1]
        for k, part in ((1, "first"), (-1, "second")):
            arrived(keys["2", n, h, fr, k], ag2_ref(n, h, fr, -k, "all"))
            ag_push(("2f", n, h, fr, k), ag2_ref(n, h, fr, -k, part), g_axis, k)

    def ag_step0(n):
        for h in (0, 1):
            for k in (1, -1):
                ag_push(("1", n, h, k), ag1_ref(n, h, 0, "all"), AXES[h][0], k)
            stage2_own(n, h, 0)

    def ag_step1(n):
        for h in (0, 1):
            for k, part in ((1, "first"), (-1, "second")):
                arrived(keys["1", n, h, k], ag1_ref(n, h, -k, "all"))
                ag_push(("1f", n, h, k), ag1_ref(n, h, -k, part), AXES[h][0], k)
                stage2_own(n, h, -k)

    def ag_step2(n):
        for h in (0, 1):
            for k, part in ((1, "first"), (-1, "second")):
                arrived(keys["1f", n, h, k], ag1_ref(n, h, 2, part))
            stage2_own(n, h, 2)
            stage2_onward(n, h, 0)

    def ag_step3(n):
        for h in (0, 1):
            for fr in (-1, 1):
                stage2_onward(n, h, fr)

    def ag_step4(n):
        for h in (0, 1):
            stage2_onward(n, h, 2)

    def ag_step5(n):
        for h in (0, 1):
            for fr in (0, -1, 1, 2):
                for k, part in ((1, "first"), (-1, "second")):
                    arrived(keys["2f", n, h, fr, k], ag2_ref(n, h, fr, 2, part))

    ag_step0(0)
    ag_step0(1)

    a_own[...] = am_ref[:, :, pl.ds(pl.multiple_of(d * SLICE, SLICE), SLICE)].reshape(2 * RANK, SLICE)
    u_pad[0, :RANK] = um_ref[0]
    u_pad[1, RANK:] = um_ref[1]
    u_pad[0, RANK:] = jnp.zeros((RANK, HID), BF16)
    u_pad[1, :RANK] = jnp.zeros((RANK, HID), BF16)
    zs[...] = jnp.zeros_like(zs)
    ad_s[...] = jnp.zeros_like(ad_s)
    tops = jnp.zeros((16, 2 * RANK), F32)
    bottoms = jnp.zeros((16, 2 * RANK), F32)
    for p in range(8):
        tokens = s_buf[1, p]
        for part in range(2):
            start = p * SLICE + part * HALF
            maps = am_ref[:, :, start : start + HALF].reshape(2 * RANK, HALF)
            value = lax.dot_general(tokens, maps, NT, preferred_element_type=F32)
            if part == 0:
                tops = tops + value
            else:
                bottoms = bottoms + value
    ad_s[:, : 2 * RANK] = jnp.concatenate([tops[:8] + bottoms[8:], jnp.zeros((8, 2 * RANK), F32)], axis=0).astype(BF16)

    ag_step1(0)
    ag_step1(1)

    ad_keys = {}
    for k, o in rels:
        ad_keys[k, o] = send(ad_s, ad_r.at[d], (peer(k, o), t))[0]
    ad_r[d] = ad_s[...]
    for k, o in rels:
        arrived(first_a2a[1, k, o], r_buf.at[1, source(k, o)])
    for u in range(4):
        left, right = unpack(1, u)
        xg[u, :, :HALF] = left
        xg[u, :, HALF:] = right

    ag_step2(0)
    ag_step2(1)
    for k, o in rels:
        arrived(ad_keys[k, o], ad_r.at[source(k, o)])
    for u in range(4):
        adn[t, u] = jnp.concatenate(
            [ad_r[2 * u].astype(F32)[:8], ad_r[2 * u + 1].astype(F32)[:8]], axis=0
        ).astype(BF16)
    adt_keys = {}
    for i in range(1, 16):
        adt_keys[i] = send(adn.at[t], adn.at[t], (d, (t + i) % 16))[0]
    ag_step3(0)
    ag_step3(1)
    ab_gather.onward()
    ag_step4(0)
    ag_step4(1)

    loads[0].wait()
    core_keys = {}

    def product1(i):
        rows = y_buf[i].reshape(256, SLICE)
        for start, size in TILES1:
            value = lax.dot_general(
                rows, wd[start : start + size, :], NT, preferred_element_type=F32
            ).reshape(16, 2, 8, size)
            for core in range(2):
                p_buf[i, core, :, start : start + size] = value[:, core].reshape(128, size).astype(BF16)
        core_keys[i] = send(p_buf.at[i, oc], q_buf.at[i], sib)[0]

    def add_rows(dst, others, lo=0, hi=128):
        def body(i, carry):
            value = None
            rows = pl.ds(pl.multiple_of(lo + i * 16, 16), 16)
            value = dst[0][rows, :].astype(F32)
            for ref, base in others:
                here = pl.ds(pl.multiple_of(lo - base + i * 16, 16), 16)
                value = value + ref[here, :].astype(F32)
            dst[1][rows, :] = value.astype(BF16)
            return carry

        lax.fori_loop(0, (hi - lo) // 16, body, 0)

    ag_step5(0)
    product1(0)
    product1(1)
    ag_step5(1)
    own = [p_buf.at[i, c] for i in range(4)]
    arrived(core_keys[0], q_buf.at[0])
    add_rows((own[0], own[0]), [(q_buf.at[0], 0)])
    k_f0 = send(p_buf.at[0, c, pl.ds(0, 64)], f_buf.at[0], up_dev)[0]
    k_f1 = send(p_buf.at[0, c, pl.ds(64, 64)], f_buf.at[1], down_dev)[0]
    product1(2)
    arrived(core_keys[1], q_buf.at[1])
    arrived(k_f0, f_buf.at[0])
    add_rows((own[1], own[1]), [(q_buf.at[1], 0), (f_buf.at[0], 0)], 0, 64)
    add_rows((own[1], own[1]), [(q_buf.at[1], 0)], 64, 128)
    k_g0 = send(p_buf.at[1, c], gz_buf.at[0], up_dev)[0]
    arrived(core_keys[2], q_buf.at[2])
    arrived(k_f1, f_buf.at[1])
    add_rows((own[2], own[2]), [(q_buf.at[2], 0)], 0, 64)
    add_rows((own[2], own[2]), [(q_buf.at[2], 0), (f_buf.at[1], 64)], 64, 128)
    k_g1 = send(p_buf.at[2, c], gz_buf.at[1], down_dev)[0]
    product1(3)
    ab_gather.last()
    ab_gather.have(0)
    ab_gather.have(3)
    ab_gather.have(1)
    for i in range(1, 16):
        arrived(adt_keys[i], adn.at[(t + 16 - i) % 16])
    arrived(core_keys[3], q_buf.at[3])
    arrived(k_g0, gz_buf.at[0])
    arrived(k_g1, gz_buf.at[1])
    add_rows((own[3], d_buf.at[z, c]), [(q_buf.at[3], 0), (gz_buf.at[0], 0), (gz_buf.at[1], 0)])

    d_gather = ZGather(
        lambda u, core: d_buf.at[u, core],
        lambda u, core, i: d_buf.at[u, core, pl.ds(64 * i, 64)],
    )
    d_gather.begin()
    loads[1].wait()
    loads[2].wait()

    rs_keys = {}

    def gradients(rel):
        u = unit(rel)
        ab_gather.release(rel)
        for core in range(2):

            def body(i, carry):
                rows = pl.ds(pl.multiple_of(i * 16, 16), 16)
                hidden = d_buf[u, core, rows, :].astype(F32)
                ab[u, 0, core, rows, :] = (hidden * ab[u, 0, core, rows, :].astype(F32)).astype(BF16)
                ab[u, 1, core, rows, :] = (hidden * ab[u, 1, core, rows, :].astype(F32)).astype(BF16)
                return carry

            lax.fori_loop(0, 8, body, 0)

    def by_token(value):
        pieces = []
        for i in range(16):
            pieces += [value[8 * i : 8 * i + 8], value[128 + 8 * i : 136 + 8 * i]]
        return jnp.concatenate(pieces, axis=0)

    def rank_terms(rel):
        u = unit(rel)
        gate = ab[u, 0].reshape(256, HID)
        up = ab[u, 1].reshape(256, HID)
        ranks = lax.dot_general(gate, u_pad[0], NT, preferred_element_type=F32) + lax.dot_general(
            up, u_pad[1], NT, preferred_element_type=F32
        )
        zs[:, u, :, : 2 * RANK] = by_token(ranks).astype(BF16).reshape(16, 16, 2 * RANK)
        return (SCALE * ranks).astype(BF16)

    def product2(rel, ranks):
        u = unit(rel)

        def body(n, carry):
            rows = pl.ds(pl.multiple_of(n * TILE2, TILE2), TILE2)
            value = lax.dot_general(ab[u, 0].reshape(256, HID), wg[rows, :], NT, preferred_element_type=F32)
            value = value + lax.dot_general(ab[u, 1].reshape(256, HID), wu[rows, :], NT, preferred_element_type=F32)
            value = value + jnp.dot(ranks, a_own[:, rows], preferred_element_type=F32)
            o_buf[u, :, :, :, rows] = by_token(value).astype(BF16).reshape(4, 4, 16, TILE2)
            return carry

        lax.fori_loop(0, SLICE // TILE2, body, 0)

    RAXES = (("y", "x"), ("x", "y"))

    def out_block(u, h, f, g, cols):
        yy, xx = (f, g) if RAXES[h][0] == "y" else (g, f)
        return o_buf.at[u, yy, xx, :, cols]

    def add_into(dst, src):
        dst[...] = (dst[...].astype(F32) + src[...].astype(F32)).astype(BF16)

    def rs_step1(rel):
        u = unit(rel)
        for h in (0, 1):
            f_axis = RAXES[h][0]
            for i, k in enumerate((1, -1)):
                rs_keys["1", rel, h, k] = send(
                    out_block(u, h, shift(f_axis, 2), pl.ds(2 * i, 2), COLS[h]),
                    r1.at[u, h, i],
                    near(f_axis, k),
                )[0]

    def rs_step2(rel):
        u = unit(rel)
        for h in (0, 1):
            f_axis = RAXES[h][0]
            for i, k in enumerate((1, -1)):
                arrived(rs_keys["1", rel, h, k], r1.at[u, h, i])
                for j in range(2):
                    add_into(out_block(u, h, shift(f_axis, k), 2 * i + j, COLS[h]), r1.at[u, h, i, j])
                rs_keys["2", rel, h, k] = send(
                    out_block(u, h, shift(f_axis, k), pl.ds(0, 4), COLS[h]),
                    r2.at[u, h, i],
                    near(f_axis, k),
                )[0]

    def half_cols(h, i):
        return pl.ds(HALF * h + 512 * i, 512)

    def rs_step3(rel):
        u = unit(rel)
        for h in (0, 1):
            f_axis, g_axis = RAXES[h]
            for i, k in enumerate((1, -1)):
                arrived(rs_keys["2", rel, h, k], r2.at[u, h, i])
            for j in range(4):
                dst = out_block(u, h, pos[f_axis], j, COLS[h])
                dst[...] = (
                    dst[...].astype(F32) + r2[u, h, 0, j].astype(F32) + r2[u, h, 1, j].astype(F32)
                ).astype(BF16)
            for i, k in enumerate((1, -1)):
                rs_keys["3", rel, h, k] = send(
                    out_block(u, h, pos[f_axis], shift(g_axis, 2), half_cols(h, i)),
                    r3.at[u, h, i],
                    near(g_axis, k),
                )[0]

    def rs_step4(rel):
        u = unit(rel)
        for h in (0, 1):
            f_axis, g_axis = RAXES[h]
            for i, k in enumerate((1, -1)):
                arrived(rs_keys["3", rel, h, k], r3.at[u, h, i])
                add_into(out_block(u, h, pos[f_axis], shift(g_axis, k), half_cols(h, i)), r3.at[u, h, i])
                rs_keys["4", rel, h, k] = send(
                    out_block(u, h, pos[f_axis], shift(g_axis, k), COLS[h]),
                    r4.at[u, h, i],
                    near(g_axis, k),
                )[0]

    last_a2a = {}

    def rs_step5(rel):
        u = unit(rel)
        halves = []
        for h in (0, 1):
            f_axis, g_axis = RAXES[h]
            for i, k in enumerate((1, -1)):
                arrived(rs_keys["4", rel, h, k], r4.at[u, h, i])
            own_block = out_block(u, h, pos[f_axis], pos[g_axis], COLS[h])[...].astype(F32)
            halves.append(own_block + r4[u, h, 0].astype(F32) + r4[u, h, 1].astype(F32))
        for core in range(2):
            rows = slice(8 * core, 8 * core + 8)
            t_buf[2 * u + core] = jnp.concatenate([halves[0][rows], halves[1][rows]], axis=0).astype(BF16)
        for o in (0, 1):
            if (rel, o) == (0, 0):
                v_buf[d] = t_buf[d]
            else:
                last_a2a[rel, o] = send(t_buf.at[peer(rel, o)], v_buf.at[d], (peer(rel, o), t))[0]

    steps = (rs_step1, rs_step2, rs_step3, rs_step4, rs_step5)

    def advance(turn):
        for s in range(5):
            i = turn - s
            if 0 <= i < 4:
                steps[s](ORDER2[i])

    def z_sum():
        for i in range(1, 16):
            arrived(z_keys[i], zr.at[(t + 16 - i) % 16])
        zr[t] = zs[t]
        total = zr[0].astype(F32)
        for i in range(1, 16):
            total = total + zr[i].astype(F32)
        turned = jnp.transpose(total.reshape(64, 128))[: 2 * RANK].astype(BF16)
        terms = jnp.dot(turned, xg[...].reshape(64, SLICE), preferred_element_type=F32)
        for i in range(16):
            ds_buf[i] = terms[:, HB * i : HB * (i + 1)].astype(BF16)
        for i in range(1, 16):
            to = (t + i) % 16
            down_keys[i] = send(ds_buf.at[to], dr_buf.at[t], (d, to))[0]
        dr_buf[t] = ds_buf[t]

    def down_sum():
        for i in range(1, 16):
            arrived(down_keys[i], dr_buf.at[(t + 16 - i) % 16])
        total = dr_buf[0].astype(F32)
        for i in range(1, 16):
            total = total + dr_buf[i].astype(F32)
        e_buf[d, t] = (total * GRAD_SCALE).astype(BF16)
        for i in range(1, 16):
            piece_keys[i] = send(e_buf.at[d, t], e_buf.at[d, t], (d, (t + i) % 16))[0]

    z_keys, down_keys, piece_keys = {}, {}, {}
    e_gather = ZGather(
        lambda u, core: e_buf.at[2 * u + core],
        lambda u, core, i: e_buf.at[2 * u + core, pl.ds(8 * i, 8)],
    )

    d_gather.have(0)
    gradients(0)
    product2(0, rank_terms(0))
    d_gather.onward()
    advance(0)
    d_gather.have(3)
    gradients(3)
    product2(3, rank_terms(3))
    d_gather.last()
    advance(1)
    d_gather.have(1)
    gradients(1)
    product2(1, rank_terms(1))
    advance(2)
    d_gather.have(2)
    ab_gather.have(2)
    gradients(2)
    ranks = rank_terms(2)
    for i in range(1, 16):
        to = (t + i) % 16
        z_keys[i] = send(zs.at[to], zr.at[t], (d, to))[0]
    product2(2, ranks)
    advance(3)
    z_sum()
    advance(4)
    down_sum()
    advance(5)
    for i in range(1, 16):
        whose = (t + 16 - i) % 16
        arrived(piece_keys[i], e_buf.at[d, whose])
    e_gather.begin()
    advance(6)

    grads_up = [jnp.zeros((2 * RANK, HID), F32), jnp.zeros((2 * RANK, HID), F32)]
    for u in range(4):
        low = adn[:, u].astype(F32)
        rows = jnp.concatenate([low[:, :8].reshape(128, HB), low[:, 8:].reshape(128, HB)], axis=0)
        turned = jnp.transpose(rows)[: 2 * RANK].astype(BF16)
        for i in range(2):
            grads_up[i] = grads_up[i] + jnp.dot(turned, ab[u, i].reshape(256, HID), preferred_element_type=F32)
    up_ref[0] = grads_up[0][:RANK] * GRAD_SCALE
    up_ref[1] = grads_up[1][RANK:] * GRAD_SCALE

    e_gather.onward()
    advance(7)
    e_gather.last()
    for k, o in rels:
        arrived(last_a2a[k, o], v_buf.at[source(k, o)])
    for p in range(8):
        value = v_buf[p]
        out_ref[0, :, p * SLICE : p * SLICE + HALF] = value[:8]
        out_ref[0, :, p * SLICE + HALF : (p + 1) * SLICE] = value[8:]
    for rel in range(4):
        e_gather.have(rel)
    for p in range(8):
        for i in range(16):
            start = p * SLICE + HB * i
            down_ref[:, start : start + HB] = e_buf[p, i].astype(F32)
    for copy in pending:
        copy.wait_send()
    assert count[0] == NSEM


def on_device(kept, grad, gate_pre, up_pre, wg, wu, wd, a_maps, u_maps):
    vmem = pl.BlockSpec(memory_space=pltpu.VMEM)
    hbm = pl.BlockSpec(memory_space=pl.ANY)
    shapes = [
        (HID, SLICE), (SLICE, HID), (SLICE, HID),
        (2, 8, 16, HALF), (2, 8, 16, HALF),
        (4, 4, 4, 16, SLICE),
        (4, 16, SLICE),
        (4, 2, 128, HID), (4, 128, HID), (2, 64, HID), (2, 128, HID), (4, 2, 128, HID),
        (4, 2, 2, 128, HID),
        (4, 4, 4, 16, SLICE),
        (4, 2, 2, 2, 16, HALF), (4, 2, 2, 4, 16, HALF), (4, 2, 2, 16, 512), (4, 2, 2, 16, HALF),
        (8, 16, HALF), (8, 16, HALF),
        (16, HB), (8, 16, HB), (16, 4, 16, HB),
        (16, 4, 16, HB), (16, 4, 16, HB),
        (16, 2 * RANK, HB), (16, 2 * RANK, HB), (8, 16, 2 * RANK, HB),
        (2 * RANK, SLICE), (2, 2 * RANK, HID),
    ]
    out, down, up = pl.pallas_call(
        kernel,
        out_shape=(
            jax.ShapeDtypeStruct((1, 8, WIDTH), BF16),
            jax.ShapeDtypeStruct((2 * RANK, WIDTH), F32),
            jax.ShapeDtypeStruct((2, RANK, HID), F32),
        ),
        in_specs=[vmem] * 7 + [hbm] * 3,
        out_specs=(vmem,) * 3,
        scratch_shapes=[pltpu.VMEM(s, BF16) for s in shapes]
        + [
            pltpu.SemaphoreType.DMA((NSEM,)),
            pltpu.SemaphoreType.DMA((NSEM,)),
            pltpu.SemaphoreType.DMA((3,)),
        ],
        compiler_params=pltpu.CompilerParams(
            collective_id=0, has_side_effects=True, vmem_limit_bytes=66_000_000
        ),
        name="gated_backward",
    )(kept, grad, gate_pre, up_pre, a_maps, u_maps, jnp.asarray(sign_table(), BF16), wd, wg, wu)
    return out, down.reshape(2, RANK, WIDTH), up


def solution(mesh):
    placed = (
        P("dp", "tensor", None),
        P("dp", "tensor", None),
        P("dp", None, "tensor"),
        P("dp", None, "tensor"),
        P("dp", "tensor"),
        P("dp", "tensor"),
        P("tensor", "dp"),
        P(),
        P(None, None, "tensor"),
    )
    return jax.shard_map(
        on_device,
        mesh=mesh,
        in_specs=placed,
        out_specs=(P("dp", "tensor", None), P(), P(None, None, "tensor")),
        check_vma=False,
    )
```

```python
import functools

import jax
import jax.numpy as jnp
import numpy as np
from jax import lax
from jax.experimental import pallas as pl
from jax.experimental.pallas import tpu as pltpu
from jax.sharding import PartitionSpec as P

F32 = jnp.float32
BF16 = jnp.bfloat16
HB = 128
WIDTH = 16384
SLICE = 2048
HALF = 1024
HID = 1664
RANK = 16
SCALE = 2.0
GRAD_SCALE = SCALE / 1024.0**0.5
ORDER1 = (2, 1, 3, 0)
ORDER2 = (0, 3, 1, 2)
TILES1 = ((0, 640), (640, 512), (1152, 512))
TILE2 = 512
NSEM = 301
NT = (((1,), (1,)), ((), ()))


def sign_table():
    index = np.arange(HB)
    common = index[:, None] & index[None, :]
    parity = np.zeros_like(common)
    for bit in range(7):
        parity += (common >> bit) & 1
    return (1 - 2 * (parity % 2)).astype(np.float32)


def kernel(
    x_hbm, dy_hbm, g_hbm, u_hbm, am_hbm, um_hbm, h_hbm, wd_hbm, wg_hbm, wu_hbm,
    v_hbm, e_hbm, up_hbm,
    x_ref, dy_ref, g_ref, u_ref, am_ref, um_ref, h_ref, up_ref, wd, wg, wu, s_buf, r_buf, y_buf, xg, p_buf, q_buf, f_buf, gz_buf, d_buf, ab, o_buf,
    r1, r2, r3, r4, t_buf, v_buf, ad_s, ad_r, adn, zs, zr, ds_buf, dr_buf, e_buf, a_own, u_pad,
    ss, rs, ws,
):
    d = lax.axis_index("dp")
    t = lax.axis_index("tensor")
    z, c = d // 2, d % 2
    oc = 1 - c
    pos = {"y": t // 4, "x": t % 4}
    count = [0]
    pending = []

    def unit(k):
        return (z + k) % 4

    zp, zm = unit(1), unit(3)
    sib = (z * 2 + oc, t)
    up_dev, down_dev = (zp * 2 + c, t), (zm * 2 + c, t)

    def near(axis, k):
        moved = dict(pos)
        moved[axis] = (pos[axis] + k) % 4
        return (d, moved["y"] * 4 + moved["x"])

    def send(src, dst, dev):
        k = count[0]
        count[0] += 1
        copy = pltpu.make_async_remote_copy(
            src_ref=src, dst_ref=dst, send_sem=ss.at[k], recv_sem=rs.at[k],
            device_id=dev, device_id_type=pl.DeviceIdType.MESH,
        )
        copy.start()
        pending.append(copy)
        return k, copy

    def arrived(k, dst):
        pltpu.make_async_remote_copy(
            src_ref=dst, dst_ref=dst, send_sem=ss.at[k], recv_sem=rs.at[k],
            device_id=sib, device_id_type=pl.DeviceIdType.MESH,
        ).wait_recv()

    def sent(copy):
        copy.wait_send()
        pending[:] = [other for other in pending if other is not copy]

    loads = {}
    for k, (name, src, dst) in enumerate((
        ("h", h_hbm, h_ref), ("g", g_hbm, g_ref), ("u", u_hbm, u_ref), ("dy", dy_hbm, dy_ref), ("x", x_hbm, x_ref),
        ("am", am_hbm, am_ref), ("um", um_hbm, um_ref), ("wd", wd_hbm, wd), ("wg", wg_hbm, wg), ("wu", wu_hbm, wu),
    )):
        loads[name] = pltpu.make_async_copy(src, dst, ws.at[k])
        if k < 7:
            loads[name].start()

    def loaded(*names):
        for name in names:
            loads[name].wait()

    barrier = pltpu.get_barrier_semaphore()
    for i in range(1, 8):
        pl.semaphore_signal(barrier, inc=1, device_id=((d + i) % 8, t), device_id_type=pl.DeviceIdType.MESH)
    for i in range(1, 16):
        pl.semaphore_signal(barrier, inc=1, device_id=(d, (t + i) % 16), device_id_type=pl.DeviceIdType.MESH)

    def rotate(src, slot):
        flat = src[0].astype(F32)
        rows = jnp.concatenate([flat[:, HB * k : HB * (k + 1)] for k in range(WIDTH // HB)], axis=0)
        turned = jnp.dot(rows.astype(BF16), h_ref[...], preferred_element_type=F32) * (1.0 / HB**0.5)
        for p in range(8):
            for j in range(8):
                first, second = 8 * (16 * p + j), 8 * (16 * p + 8 + j)
                s_buf[slot, p, :, HB * j : HB * (j + 1)] = jnp.concatenate(
                    [turned[first : first + 8], turned[second : second + 8]], axis=0
                ).astype(BF16)

    rels = [(k, o) for k in (2, 1, 3, 0) for o in (0, 1) if (k, o) != (0, 0)]

    def peer(k, o):
        return unit(k) * 2 + (oc if o else c)

    def source(k, o):
        return unit((4 - k) % 4) * 2 + (oc if o else c)

    def factors(i, carry):
        rows = pl.ds(pl.multiple_of(i * 16, 16), 16)
        gate = g_ref[0, rows, :].astype(F32)
        up = u_ref[0, rows, :].astype(F32)
        squash = 1.0 / (1.0 + jnp.exp(-gate))
        ab[z, 0, c, rows, :] = (up * squash * (1.0 + gate * (1.0 - squash))).astype(BF16)
        ab[z, 1, c, rows, :] = (gate * squash).astype(BF16)
        return carry

    first_a2a = {}

    def exchange(slot):
        for k, o in rels:
            first_a2a[slot, k, o] = send(
                s_buf.at[slot, peer(k, o)], r_buf.at[slot, d], (peer(k, o), t)
            )[0]
        r_buf[slot, d] = s_buf[slot, d]

    loaded("g", "u")
    lax.fori_loop(0, 8, factors, 0)
    loaded("h", "dy")
    rotate(dy_ref, 0)
    pl.semaphore_wait(barrier, 22)
    exchange(0)

    class ZGather:
        def __init__(self, whole, half):
            self.whole, self.half = whole, half
            self.copies = {0: [], 1: [], 2: [], 3: []}
            self.k_from = {}

        def begin(self):
            self.k_up = self.push(0, self.whole(z, c), up_dev)
            self.k_down = self.push(0, self.whole(z, c), down_dev)
            self.k_from[0] = self.push(0, self.whole(z, c), sib)

        def push(self, owner, ref, dev):
            k, copy = send(ref, ref, dev)
            self.copies[owner].append(copy)
            return k

        def across(self):
            arrived(self.k_up, self.whole(zm, c))
            self.k_from[3] = self.push(3, self.whole(zm, c), sib)
            arrived(self.k_down, self.whole(zp, c))
            self.k_from[1] = self.push(1, self.whole(zp, c), sib)

        def pass_up(self):
            self.k_f0 = self.push(3, self.half(zm, c, 0), up_dev)

        def pass_down(self):
            self.k_f1 = self.push(1, self.half(zp, c, 1), down_dev)

        def last(self):
            arrived(self.k_f0, self.half(unit(2), c, 0))
            arrived(self.k_f1, self.half(unit(2), c, 1))
            self.k_from[2] = self.push(2, self.whole(unit(2), c), sib)

        def have(self, rel):
            arrived(self.k_from[rel], self.whole(unit(rel), oc))

        def release(self, rel):
            for copy in self.copies[rel]:
                sent(copy)
            self.copies[rel] = []

    ab_gather = ZGather(
        lambda u, core: ab.at[u, :, core],
        lambda u, core, i: ab.at[u, i, core],
    )
    ab_gather.begin()
    loaded("x")
    rotate(x_ref, 1)
    exchange(1)

    def unpack(slot, u):
        low = r_buf[slot, 2 * u].astype(F32)
        high = r_buf[slot, 2 * u + 1].astype(F32)
        left = jnp.concatenate([low[:8], high[:8]], axis=0).astype(BF16)
        right = jnp.concatenate([low[8:], high[8:]], axis=0).astype(BF16)
        return left, right

    for k, o in rels:
        arrived(first_a2a[0, k, o], r_buf.at[0, source(k, o)])
    for i, rel in enumerate(ORDER1):
        left, right = unpack(0, unit(rel))
        y_buf[i, pos["y"], pos["x"], :, :HALF] = left
        y_buf[i, pos["y"], pos["x"], :, HALF:] = right

    AXES = (("x", "y"), ("y", "x"))

    def block(buf, lead, h, f, g, cols):
        yy, xx = (g, f) if AXES[h][0] == "x" else (f, g)
        return buf.at[lead, yy, xx, :, cols]

    COLS = (pl.ds(0, HALF), pl.ds(HALF, HALF))
    chunks = ((0, 1), (1, 2), (3, 1))
    keys = {}

    def shift(axis, k):
        return (pos[axis] + k) % 4

    def half_cols(h, i):
        return pl.ds(HALF * h + 512 * i, 512)

    def cols_of(h, part):
        return COLS[h] if part == "all" else half_cols(h, 0 if part == "first" else 1)

    def ag1_ref(n, h, fr, part):
        f_axis, g_axis = AXES[h]
        return block(y_buf, pl.ds(*chunks[n]), h, shift(f_axis, fr), pos[g_axis], cols_of(h, part))

    def ag2_ref(n, h, fr, gr, part):
        f_axis, g_axis = AXES[h]
        return block(y_buf, pl.ds(*chunks[n]), h, shift(f_axis, fr), shift(g_axis, gr), cols_of(h, part))

    def ag_push(key, ref, axis, k):
        keys[key] = send(ref, ref, near(axis, k))[0]

    def stage2_own(n, h, fr):
        g_axis = AXES[h][1]
        for k in (1, -1):
            ag_push(("2", n, h, fr, k), ag2_ref(n, h, fr, 0, "all"), g_axis, k)

    def stage2_onward(n, h, fr):
        g_axis = AXES[h][1]
        for k, part in ((1, "first"), (-1, "second")):
            arrived(keys["2", n, h, fr, k], ag2_ref(n, h, fr, -k, "all"))
            ag_push(("2f", n, h, fr, k), ag2_ref(n, h, fr, -k, part), g_axis, k)

    def ag_step0(n):
        for h in (0, 1):
            for k in (1, -1):
                ag_push(("1", n, h, k), ag1_ref(n, h, 0, "all"), AXES[h][0], k)
            stage2_own(n, h, 0)

    def ag_step1(n):
        for h in (0, 1):
            for k, part in ((1, "first"), (-1, "second")):
                arrived(keys["1", n, h, k], ag1_ref(n, h, -k, "all"))
                ag_push(("1f", n, h, k), ag1_ref(n, h, -k, part), AXES[h][0], k)
                stage2_own(n, h, -k)

    def ag_step2(n):
        for h in (0, 1):
            for k, part in ((1, "first"), (-1, "second")):
                arrived(keys["1f", n, h, k], ag1_ref(n, h, 2, part))
            stage2_own(n, h, 2)
            stage2_onward(n, h, 0)

    def ag_step3(n):
        for h in (0, 1):
            for fr in (-1, 1):
                stage2_onward(n, h, fr)

    def ag_step4(n):
        for h in (0, 1):
            stage2_onward(n, h, 2)

    def ag_step5(n):
        for h in (0, 1):
            for fr in (0, -1, 1, 2):
                for k, part in ((1, "first"), (-1, "second")):
                    arrived(keys["2f", n, h, fr, k], ag2_ref(n, h, fr, 2, part))

    ag_step0(0)
    loads["wd"].start()
    ag_step1(0)
    ag_step0(1)
    ag_step2(0)
    ag_step3(0)
    ag_step1(1)
    ag_step4(0)
    ag_step2(1)
    loaded("am", "um", "wd")

    a_own[...] = am_ref[:, :, pl.ds(pl.multiple_of(d * SLICE, SLICE), SLICE)].reshape(2 * RANK, SLICE)
    u_pad[0, :RANK] = um_ref[0]
    u_pad[1, RANK:] = um_ref[1]
    u_pad[0, RANK:] = jnp.zeros((RANK, HID), BF16)
    u_pad[1, :RANK] = jnp.zeros((RANK, HID), BF16)
    zs[...] = jnp.zeros_like(zs)
    ad_s[...] = jnp.zeros_like(ad_s)
    def adapter_down():
        tops = jnp.zeros((16, 2 * RANK), F32)
        bottoms = jnp.zeros((16, 2 * RANK), F32)
        for p in range(8):
            tokens = s_buf[1, p]
            for part in range(2):
                start = p * SLICE + part * HALF
                maps = am_ref[:, :, start : start + HALF].reshape(2 * RANK, HALF)
                value = lax.dot_general(tokens, maps, NT, preferred_element_type=F32)
                if part == 0:
                    tops = tops + value
                else:
                    bottoms = bottoms + value
        ad_s[:, : 2 * RANK] = jnp.concatenate([tops[:8] + bottoms[8:], jnp.zeros((8, 2 * RANK), F32)], axis=0).astype(BF16)

    def adapters_out():
        for k, o in rels:
            ad_keys[k, o] = send(ad_s, ad_r.at[d], (peer(k, o), t))[0]
        ad_r[d] = ad_s[...]

    def adapters_on():
        for k, o in rels:
            arrived(ad_keys[k, o], ad_r.at[source(k, o)])
        for u in range(4):
            adn[t, u] = jnp.concatenate(
                [ad_r[2 * u].astype(F32)[:8], ad_r[2 * u + 1].astype(F32)[:8]], axis=0
            ).astype(BF16)
        for i in range(1, 16):
            adt_keys[i] = send(adn.at[t], adn.at[t], (d, (t + i) % 16))[0]

    def inputs_in():
        for k, o in rels:
            arrived(first_a2a[1, k, o], r_buf.at[1, source(k, o)])
        for u in range(4):
            left, right = unpack(1, u)
            xg[u, :, :HALF] = left
            xg[u, :, HALF:] = right

    ad_keys, adt_keys, core_keys = {}, {}, {}

    def product1(i):
        rows = y_buf[i].reshape(256, SLICE)
        for start, size in TILES1:
            value = lax.dot_general(
                rows, wd[start : start + size, :], NT, preferred_element_type=F32
            ).reshape(16, 2, 8, size)
            for core in range(2):
                p_buf[i, core, :, start : start + size] = value[:, core].reshape(128, size).astype(BF16)
        core_keys[i] = send(p_buf.at[i, oc], q_buf.at[i], sib)[0]

    def add_rows(dst, others, lo=0, hi=128):
        def body(i, carry):
            value = None
            rows = pl.ds(pl.multiple_of(lo + i * 16, 16), 16)
            value = dst[0][rows, :].astype(F32)
            for ref, base in others:
                here = pl.ds(pl.multiple_of(lo - base + i * 16, 16), 16)
                value = value + ref[here, :].astype(F32)
            dst[1][rows, :] = value.astype(BF16)
            return carry

        lax.fori_loop(0, (hi - lo) // 16, body, 0)

    own = [p_buf.at[i, c] for i in range(4)]
    ag_step5(0)
    product1(0)
    ag_step0(2)
    loads["wg"].start()
    ag_step3(1)
    ag_step1(2)
    arrived(core_keys[0], q_buf.at[0])
    add_rows((own[0], own[0]), [(q_buf.at[0], 0)])
    k_f0 = send(p_buf.at[0, c, pl.ds(0, 64)], f_buf.at[0], up_dev)[0]
    k_f1 = send(p_buf.at[0, c, pl.ds(64, 64)], f_buf.at[1], down_dev)[0]
    ag_step4(1)
    ag_step2(2)
    adapter_down()
    adapters_out()
    ag_step3(2)
    loads["wu"].start()
    ag_step5(1)
    product1(1)
    ag_step4(2)
    product1(2)
    arrived(core_keys[1], q_buf.at[1])
    arrived(k_f0, f_buf.at[0])
    add_rows((own[1], own[1]), [(q_buf.at[1], 0), (f_buf.at[0], 0)], 0, 64)
    add_rows((own[1], own[1]), [(q_buf.at[1], 0)], 64, 128)
    k_g0 = send(p_buf.at[1, c], gz_buf.at[0], up_dev)[0]
    arrived(core_keys[2], q_buf.at[2])
    arrived(k_f1, f_buf.at[1])
    add_rows((own[2], own[2]), [(q_buf.at[2], 0)], 0, 64)
    add_rows((own[2], own[2]), [(q_buf.at[2], 0), (f_buf.at[1], 64)], 64, 128)
    k_g1 = send(p_buf.at[2, c], gz_buf.at[1], down_dev)[0]
    ag_step5(2)
    product1(3)
    adapters_on()
    inputs_in()
    loaded("wg", "wu")
    arrived(core_keys[3], q_buf.at[3])
    add_rows((own[3], own[3]), [(q_buf.at[3], 0)])
    ab_gather.across()
    for rel in (0, 3, 1):
        ab_gather.have(rel)
        ab_gather.release(rel)
    arrived(k_g0, gz_buf.at[0])
    arrived(k_g1, gz_buf.at[1])
    add_rows((own[3], d_buf.at[z, c]), [(gz_buf.at[0], 0), (gz_buf.at[1], 0)])

    d_gather = ZGather(
        lambda u, core: d_buf.at[u, core],
        None,
    )
    d_gather.begin()

    rs_keys = {}

    def gradients(rel):
        u = unit(rel)
        for core in range(2):

            def body(i, carry):
                rows = pl.ds(pl.multiple_of(i * 16, 16), 16)
                hidden = d_buf[u, core, rows, :].astype(F32)
                ab[u, 0, core, rows, :] = (hidden * ab[u, 0, core, rows, :].astype(F32)).astype(BF16)
                ab[u, 1, core, rows, :] = (hidden * ab[u, 1, core, rows, :].astype(F32)).astype(BF16)
                return carry

            lax.fori_loop(0, 8, body, 0)

    def by_token(value):
        pieces = []
        for i in range(16):
            pieces += [value[8 * i : 8 * i + 8], value[128 + 8 * i : 136 + 8 * i]]
        return jnp.concatenate(pieces, axis=0)

    def rank_terms(rel):
        u = unit(rel)
        gate = ab[u, 0].reshape(256, HID)
        up = ab[u, 1].reshape(256, HID)
        ranks = lax.dot_general(gate, u_pad[0], NT, preferred_element_type=F32) + lax.dot_general(
            up, u_pad[1], NT, preferred_element_type=F32
        )
        zs[:, u, :, : 2 * RANK] = by_token(ranks).astype(BF16).reshape(16, 16, 2 * RANK)
        return (SCALE * ranks).astype(BF16)

    def product2(rel, ranks, h):
        u = unit(rel)

        def body(n, carry):
            rows = pl.ds(pl.multiple_of(HALF * h + n * TILE2, TILE2), TILE2)
            value = lax.dot_general(ab[u, 0].reshape(256, HID), wg[rows, :], NT, preferred_element_type=F32)
            value = value + lax.dot_general(ab[u, 1].reshape(256, HID), wu[rows, :], NT, preferred_element_type=F32)
            value = value + jnp.dot(ranks, a_own[:, rows], preferred_element_type=F32)
            o_buf[u, :, :, :, rows] = by_token(value).astype(BF16).reshape(4, 4, 16, TILE2)
            return carry

        lax.fori_loop(0, HALF // TILE2, body, 0)

    RAXES = (("y", "x"), ("x", "y"))

    def out_block(u, h, f, g, cols):
        yy, xx = (f, g) if RAXES[h][0] == "y" else (g, f)
        return o_buf.at[u, yy, xx, :, cols]

    def add_into(dst, src):
        dst[...] = (dst[...].astype(F32) + src[...].astype(F32)).astype(BF16)

    def rs_step1(rel, h):
        u = unit(rel)
        f_axis = RAXES[h][0]
        for i, k in enumerate((1, -1)):
            rs_keys["1", rel, h, k] = send(
                out_block(u, h, shift(f_axis, 2), pl.ds(2 * i, 2), COLS[h]),
                r1.at[u, h, i],
                near(f_axis, k),
            )[0]

    def rs_step2(rel, h):
        u = unit(rel)
        f_axis = RAXES[h][0]
        for i, k in enumerate((1, -1)):
            arrived(rs_keys["1", rel, h, k], r1.at[u, h, i])
            for j in range(2):
                add_into(out_block(u, h, shift(f_axis, k), 2 * i + j, COLS[h]), r1.at[u, h, i, j])
            rs_keys["2", rel, h, k] = send(
                out_block(u, h, shift(f_axis, k), pl.ds(0, 4), COLS[h]),
                r2.at[u, h, i],
                near(f_axis, k),
            )[0]

    def rs_step3(rel, h):
        u = unit(rel)
        f_axis, g_axis = RAXES[h]
        for i, k in enumerate((1, -1)):
            arrived(rs_keys["2", rel, h, k], r2.at[u, h, i])
        for j in range(4):
            dst = out_block(u, h, pos[f_axis], j, COLS[h])
            dst[...] = (
                dst[...].astype(F32) + r2[u, h, 0, j].astype(F32) + r2[u, h, 1, j].astype(F32)
            ).astype(BF16)
        for i, k in enumerate((1, -1)):
            rs_keys["3", rel, h, k] = send(
                out_block(u, h, pos[f_axis], shift(g_axis, 2), half_cols(h, i)),
                r3.at[u, h, i],
                near(g_axis, k),
            )[0]

    def rs_step4(rel, h):
        u = unit(rel)
        f_axis, g_axis = RAXES[h]
        for i, k in enumerate((1, -1)):
            arrived(rs_keys["3", rel, h, k], r3.at[u, h, i])
            add_into(out_block(u, h, pos[f_axis], shift(g_axis, k), half_cols(h, i)), r3.at[u, h, i])
            rs_keys["4", rel, h, k] = send(
                out_block(u, h, pos[f_axis], shift(g_axis, k), COLS[h]),
                r4.at[u, h, i],
                near(g_axis, k),
            )[0]

    last_a2a = {}

    def rs_step5(rel, h):
        if h == 0:
            return
        u = unit(rel)
        halves = []
        for h in (0, 1):
            f_axis, g_axis = RAXES[h]
            for i, k in enumerate((1, -1)):
                arrived(rs_keys["4", rel, h, k], r4.at[u, h, i])
            own_block = out_block(u, h, pos[f_axis], pos[g_axis], COLS[h])[...].astype(F32)
            halves.append(own_block + r4[u, h, 0].astype(F32) + r4[u, h, 1].astype(F32))
        for core in range(2):
            rows = slice(8 * core, 8 * core + 8)
            t_buf[2 * u + core] = jnp.concatenate([halves[0][rows], halves[1][rows]], axis=0).astype(BF16)
        for o in (0, 1):
            if (rel, o) == (0, 0):
                v_buf[d] = t_buf[d]
            else:
                last_a2a[rel, o] = send(t_buf.at[peer(rel, o)], v_buf.at[d], (peer(rel, o), t))[0]

    steps = (rs_step1, rs_step2, rs_step3, rs_step4, rs_step5)

    items = [(rel, h) for rel in ORDER2 for h in (0, 1)]

    def advance(turn):
        for k in range(5):
            if 0 <= turn - k < 8:
                steps[k](*items[turn - k])

    def z_sum():
        for i in range(1, 16):
            arrived(z_keys[i], zr.at[(t + 16 - i) % 16])
        zr[t] = zs[t]
        total = zr[0].astype(F32)
        for i in range(1, 16):
            total = total + zr[i].astype(F32)
        turned = jnp.transpose(total.reshape(64, 128))[: 2 * RANK].astype(BF16)
        terms = jnp.dot(turned, xg[...].reshape(64, SLICE), preferred_element_type=F32)
        for i in range(16):
            ds_buf[i] = terms[:, HB * i : HB * (i + 1)].astype(BF16)
        for i in range(1, 16):
            to = (t + i) % 16
            down_keys[i] = send(ds_buf.at[to], dr_buf.at[t], (d, to))[0]
        dr_buf[t] = ds_buf[t]

    def down_sum():
        for i in range(1, 16):
            arrived(down_keys[i], dr_buf.at[(t + 16 - i) % 16])
        total = dr_buf[0].astype(F32)
        for i in range(1, 16):
            total = total + dr_buf[i].astype(F32)
        e_buf[d, t] = (total * GRAD_SCALE).astype(BF16)
        for i in range(1, 16):
            piece_keys[i] = send(e_buf.at[d, t], e_buf.at[d, t], (d, (t + i) % 16))[0]

    z_keys, down_keys, piece_keys = {}, {}, {}
    e_gather = ZGather(
        lambda u, core: e_buf.at[2 * u + core],
        lambda u, core, i: e_buf.at[2 * u + core, pl.ds(8 * i, 8)],
    )

    grads_up = [jnp.zeros((2 * RANK, HID), F32), jnp.zeros((2 * RANK, HID), F32)]

    def up_grads(rel):
        u = unit(rel)
        low = adn[:, u].astype(F32)
        rows = jnp.concatenate([low[:, :8].reshape(128, HB), low[:, 8:].reshape(128, HB)], axis=0)
        turned = jnp.transpose(rows)[: 2 * RANK].astype(BF16)
        for i in range(2):
            grads_up[i] = grads_up[i] + jnp.dot(turned, ab[u, i].reshape(256, HID), preferred_element_type=F32)

    d_gather.have(0)
    gradients(0)
    ranks = rank_terms(0)
    product2(0, ranks, 0)
    advance(0)
    product2(0, ranks, 1)
    advance(1)
    d_gather.across()
    d_gather.have(3)
    gradients(3)
    ab_gather.pass_up()
    d_gather.have(1)
    gradients(1)
    ab_gather.pass_down()
    ranks = rank_terms(3)
    product2(3, ranks, 0)
    advance(2)
    product2(3, ranks, 1)
    advance(3)
    ranks = rank_terms(1)
    product2(1, ranks, 0)
    advance(4)
    product2(1, ranks, 1)
    ab_gather.last()
    advance(5)
    ab_gather.have(2)
    ranks = rank_terms(2)
    for i in range(1, 16):
        to = (t + i) % 16
        z_keys[i] = send(zs.at[to], zr.at[t], (d, to))[0]
    product2(2, ranks, 0)
    advance(6)
    z_sum()
    product2(2, ranks, 1)
    advance(7)
    down_sum()
    for i in range(1, 16):
        arrived(adt_keys[i], adn.at[(t + 16 - i) % 16])
    up_grads(0)
    up_grads(3)
    advance(8)
    for i in range(1, 16):
        arrived(piece_keys[i], e_buf.at[d, (t + 16 - i) % 16])
    e_gather.begin()
    advance(9)
    up_grads(1)
    up_grads(2)
    up_ref[0] = grads_up[0][:RANK] * GRAD_SCALE
    up_ref[1] = grads_up[1][RANK:] * GRAD_SCALE
    stores = [pltpu.make_async_copy(up_ref, up_hbm, ws.at[0])]
    stores[0].start()
    advance(10)
    e_gather.across()
    e_gather.pass_up()
    e_gather.pass_down()
    advance(11)
    e_gather.last()
    for rel in range(4):
        e_gather.have(rel)
    stores.append(pltpu.make_async_copy(e_buf, e_hbm, ws.at[1]))
    stores[1].start()
    for k, o in rels:
        arrived(last_a2a[k, o], v_buf.at[source(k, o)])
    stores.append(pltpu.make_async_copy(v_buf, v_hbm, ws.at[2]))
    stores[2].start()
    for copy in pending:
        copy.wait_send()
    for copy in stores:
        copy.wait()
    assert count[0] == NSEM


def finish(v_ref, e_ref, up_in, out_ref, down_ref, up_ref):
    for p in range(8):
        value = v_ref[p]
        out_ref[0, :, p * SLICE : p * SLICE + HALF] = value[:8]
        out_ref[0, :, p * SLICE + HALF : (p + 1) * SLICE] = value[8:]
        for i in range(16):
            start = p * SLICE + HB * i
            down_ref[:, start : start + HB] = e_ref[p, i].astype(F32)
    up_ref[...] = up_in[...]


def on_device(kept, grad, gate_pre, up_pre, wg, wu, wd, a_maps, u_maps):
    vmem = pl.BlockSpec(memory_space=pltpu.VMEM)
    hbm = pl.BlockSpec(memory_space=pl.ANY)
    operands = [
        (1, 8, WIDTH), (1, 8, WIDTH), (1, 128, HID), (1, 128, HID), (2, RANK, WIDTH), (2, RANK, HID), (HB, HB),
    ]
    shapes = [
        (HID, SLICE), (SLICE, HID), (SLICE, HID),
        (2, 8, 16, HALF), (2, 8, 16, HALF),
        (4, 4, 4, 16, SLICE),
        (4, 16, SLICE),
        (4, 2, 128, HID), (4, 128, HID), (2, 64, HID), (2, 128, HID), (4, 2, 128, HID),
        (4, 2, 2, 128, HID),
        (4, 4, 4, 16, SLICE),
        (4, 2, 2, 2, 16, HALF), (4, 2, 2, 4, 16, HALF), (4, 2, 2, 16, 512), (4, 2, 2, 16, HALF),
        (8, 16, HALF), (8, 16, HALF),
        (16, HB), (8, 16, HB), (16, 4, 16, HB),
        (16, 4, 16, HB), (16, 4, 16, HB),
        (16, 2 * RANK, HB), (16, 2 * RANK, HB), (8, 16, 2 * RANK, HB),
        (2 * RANK, SLICE), (2, 2 * RANK, HID),
    ]
    results = pl.pallas_call(
        kernel,
        out_shape=(
            jax.ShapeDtypeStruct((8, 16, HALF), BF16),
            jax.ShapeDtypeStruct((8, 16, 2 * RANK, HB), BF16),
            jax.ShapeDtypeStruct((2, RANK, HID), F32),
        ),
        in_specs=[hbm] * 10,
        out_specs=(hbm,) * 3,
        scratch_shapes=[pltpu.VMEM(s, BF16) for s in operands]
        + [pltpu.VMEM((2, RANK, HID), F32)]
        + [pltpu.VMEM(s, BF16) for s in shapes]
        + [
            pltpu.SemaphoreType.DMA((NSEM,)),
            pltpu.SemaphoreType.DMA((NSEM,)),
            pltpu.SemaphoreType.DMA((10,)),
        ],
        compiler_params=pltpu.CompilerParams(
            collective_id=0, has_side_effects=True, vmem_limit_bytes=66_000_000
        ),
        name="gated_backward",
    )(kept, grad, gate_pre, up_pre, a_maps, u_maps, jnp.asarray(sign_table(), BF16), wd, wg, wu)
    out, down, up = pl.pallas_call(
        finish,
        out_shape=(
            jax.ShapeDtypeStruct((1, 8, WIDTH), BF16),
            jax.ShapeDtypeStruct((2 * RANK, WIDTH), F32),
            jax.ShapeDtypeStruct((2, RANK, HID), F32),
        ),
        in_specs=[vmem] * 3,
        out_specs=(vmem,) * 3,
        name="finish",
    )(*results)
    return out, down.reshape(2, RANK, WIDTH), up


def solution(mesh):
    placed = (
        P("dp", "tensor", None),
        P("dp", "tensor", None),
        P("dp", None, "tensor"),
        P("dp", None, "tensor"),
        P("dp", "tensor"),
        P("dp", "tensor"),
        P("tensor", "dp"),
        P(),
        P(None, None, "tensor"),
    )
    return jax.shard_map(
        on_device,
        mesh=mesh,
        in_specs=placed,
        out_specs=(P("dp", "tensor", None), P(), P(None, None, "tensor")),
        check_vma=False,
    )
```

```python
import functools

import jax
import jax.numpy as jnp
import numpy as np
from jax import lax
from jax.experimental import pallas as pl
from jax.experimental.pallas import tpu as pltpu
from jax.sharding import PartitionSpec as P

F32 = jnp.float32
BF16 = jnp.bfloat16
HB = 128
WIDTH = 16384
SLICE = 2048
HALF = 1024
HID = 1664
RANK = 16
SCALE = 2.0
GRAD_SCALE = SCALE / 1024.0**0.5
ORDER1 = (2, 1, 3, 0)
ORDER2 = (0, 3, 1, 2)
TILES1 = ((0, 640), (640, 512), (1152, 512))
TILE2 = 512
NSEM = 301
NT = (((1,), (1,)), ((), ()))


def sign_table():
    index = np.arange(HB)
    common = index[:, None] & index[None, :]
    parity = np.zeros_like(common)
    for bit in range(7):
        parity += (common >> bit) & 1
    return (1 - 2 * (parity % 2)).astype(np.float32)


def kernel(
    x_hbm, dy_hbm, g_hbm, u_hbm, am_hbm, um_hbm, h_hbm, wd_hbm, wg_hbm, wu_hbm,
    v_hbm, e_hbm, up_hbm,
    x_ref, dy_ref, g_ref, u_ref, am_ref, um_ref, h_ref, up_ref, wd, wg, wu, s_buf, r_buf, y_buf, xg, p_buf, q_buf, f_buf, gz_buf, d_buf, ab, o_buf,
    r1, r2, r3, r4, t_buf, v_buf, ad_s, ad_r, adn, zs, zr, ds_buf, dr_buf, e_buf, a_own, u_pad,
    ss, rs, ws,
):
    d = lax.axis_index("dp")
    t = lax.axis_index("tensor")
    z, c = d // 2, d % 2
    oc = 1 - c
    pos = {"y": t // 4, "x": t % 4}
    count = [0]
    pending = []

    def unit(k):
        return (z + k) % 4

    zp, zm = unit(1), unit(3)
    sib = (z * 2 + oc, t)
    up_dev, down_dev = (zp * 2 + c, t), (zm * 2 + c, t)

    def near(axis, k):
        moved = dict(pos)
        moved[axis] = (pos[axis] + k) % 4
        return (d, moved["y"] * 4 + moved["x"])

    def send(src, dst, dev):
        k = count[0]
        count[0] += 1
        copy = pltpu.make_async_remote_copy(
            src_ref=src, dst_ref=dst, send_sem=ss.at[k], recv_sem=rs.at[k],
            device_id=dev, device_id_type=pl.DeviceIdType.MESH,
        )
        copy.start()
        pending.append(copy)
        return k, copy

    def arrived(k, dst):
        pltpu.make_async_remote_copy(
            src_ref=dst, dst_ref=dst, send_sem=ss.at[k], recv_sem=rs.at[k],
            device_id=sib, device_id_type=pl.DeviceIdType.MESH,
        ).wait_recv()

    def sent(copy):
        copy.wait_send()
        pending[:] = [other for other in pending if other is not copy]

    loads = {}
    for k, (name, src, dst) in enumerate((
        ("h", h_hbm, h_ref), ("g", g_hbm, g_ref), ("u", u_hbm, u_ref), ("dy", dy_hbm, dy_ref), ("x", x_hbm, x_ref),
        ("am", am_hbm, am_ref), ("um", um_hbm, um_ref), ("wd", wd_hbm, wd), ("wg", wg_hbm, wg), ("wu", wu_hbm, wu),
    )):
        loads[name] = pltpu.make_async_copy(src, dst, ws.at[k])
        if k < 7:
            loads[name].start()

    def loaded(*names):
        for name in names:
            loads[name].wait()

    barrier = pltpu.get_barrier_semaphore()
    for i in range(1, 8):
        pl.semaphore_signal(barrier, inc=1, device_id=((d + i) % 8, t), device_id_type=pl.DeviceIdType.MESH)
    for i in range(1, 16):
        pl.semaphore_signal(barrier, inc=1, device_id=(d, (t + i) % 16), device_id_type=pl.DeviceIdType.MESH)

    def rotate(src, slot):
        flat = src[0].astype(F32)
        rows = jnp.concatenate([flat[:, HB * k : HB * (k + 1)] for k in range(WIDTH // HB)], axis=0)
        turned = jnp.dot(rows.astype(BF16), h_ref[...], preferred_element_type=F32) * (1.0 / HB**0.5)
        for p in range(8):
            for j in range(8):
                first, second = 8 * (16 * p + j), 8 * (16 * p + 8 + j)
                s_buf[slot, p, :, HB * j : HB * (j + 1)] = jnp.concatenate(
                    [turned[first : first + 8], turned[second : second + 8]], axis=0
                ).astype(BF16)

    rels = [(k, o) for k in (2, 1, 3, 0) for o in (0, 1) if (k, o) != (0, 0)]

    def peer(k, o):
        return unit(k) * 2 + (oc if o else c)

    def source(k, o):
        return unit((4 - k) % 4) * 2 + (oc if o else c)

    def factors(i, carry):
        rows = pl.ds(pl.multiple_of(i * 16, 16), 16)
        gate = g_ref[0, rows, :].astype(F32)
        up = u_ref[0, rows, :].astype(F32)
        squash = 1.0 / (1.0 + jnp.exp(-gate))
        ab[z, 0, c, rows, :] = (up * squash * (1.0 + gate * (1.0 - squash))).astype(BF16)
        ab[z, 1, c, rows, :] = (gate * squash).astype(BF16)
        return carry

    first_a2a = {}

    def exchange(slot):
        for k, o in rels:
            first_a2a[slot, k, o] = send(
                s_buf.at[slot, peer(k, o)], r_buf.at[slot, d], (peer(k, o), t)
            )[0]
        r_buf[slot, d] = s_buf[slot, d]

    loaded("h", "dy")
    rotate(dy_ref, 0)
    pl.semaphore_wait(barrier, 22)
    exchange(0)
    loaded("g", "u")
    lax.fori_loop(0, 8, factors, 0)

    class ZGather:
        def __init__(self, whole, half):
            self.whole, self.half = whole, half
            self.copies = {0: [], 1: [], 2: [], 3: []}
            self.k_from = {}

        def begin(self):
            self.k_up = self.push(0, self.whole(z, c), up_dev)
            self.k_down = self.push(0, self.whole(z, c), down_dev)
            self.k_from[0] = self.push(0, self.whole(z, c), sib)

        def push(self, owner, ref, dev):
            k, copy = send(ref, ref, dev)
            self.copies[owner].append(copy)
            return k

        def across(self):
            arrived(self.k_up, self.whole(zm, c))
            self.k_from[3] = self.push(3, self.whole(zm, c), sib)
            arrived(self.k_down, self.whole(zp, c))
            self.k_from[1] = self.push(1, self.whole(zp, c), sib)

        def pass_up(self):
            self.k_f0 = self.push(3, self.half(zm, c, 0), up_dev)

        def pass_down(self):
            self.k_f1 = self.push(1, self.half(zp, c, 1), down_dev)

        def last(self):
            arrived(self.k_f0, self.half(unit(2), c, 0))
            arrived(self.k_f1, self.half(unit(2), c, 1))
            self.k_from[2] = self.push(2, self.whole(unit(2), c), sib)

        def have(self, rel):
            arrived(self.k_from[rel], self.whole(unit(rel), oc))

        def release(self, rel):
            for copy in self.copies[rel]:
                sent(copy)
            self.copies[rel] = []

    ab_gather = ZGather(
        lambda u, core: ab.at[u, :, core],
        lambda u, core, i: ab.at[u, i, core],
    )
    ab_gather.begin()

    def unpack(slot, u):
        low = r_buf[slot, 2 * u].astype(F32)
        high = r_buf[slot, 2 * u + 1].astype(F32)
        left = jnp.concatenate([low[:8], high[:8]], axis=0).astype(BF16)
        right = jnp.concatenate([low[8:], high[8:]], axis=0).astype(BF16)
        return left, right

    for k, o in rels:
        arrived(first_a2a[0, k, o], r_buf.at[0, source(k, o)])
    for i, rel in enumerate(ORDER1):
        left, right = unpack(0, unit(rel))
        y_buf[i, pos["y"], pos["x"], :, :HALF] = left
        y_buf[i, pos["y"], pos["x"], :, HALF:] = right

    AXES = (("x", "y"), ("y", "x"))

    def block(buf, lead, h, f, g, cols):
        yy, xx = (g, f) if AXES[h][0] == "x" else (f, g)
        return buf.at[lead, yy, xx, :, cols]

    COLS = (pl.ds(0, HALF), pl.ds(HALF, HALF))
    chunks = ((0, 1), (1, 2), (3, 1))
    keys = {}

    def shift(axis, k):
        return (pos[axis] + k) % 4

    def half_cols(h, i):
        return pl.ds(HALF * h + 512 * i, 512)

    def cols_of(h, part):
        return COLS[h] if part == "all" else half_cols(h, 0 if part == "first" else 1)

    def ag1_ref(n, h, fr, part):
        f_axis, g_axis = AXES[h]
        return block(y_buf, pl.ds(*chunks[n]), h, shift(f_axis, fr), pos[g_axis], cols_of(h, part))

    def ag2_ref(n, h, fr, gr, part):
        f_axis, g_axis = AXES[h]
        return block(y_buf, pl.ds(*chunks[n]), h, shift(f_axis, fr), shift(g_axis, gr), cols_of(h, part))

    def ag_push(key, ref, axis, k):
        keys[key] = send(ref, ref, near(axis, k))[0]

    def stage2_own(n, h, fr):
        g_axis = AXES[h][1]
        for k in (1, -1):
            ag_push(("2", n, h, fr, k), ag2_ref(n, h, fr, 0, "all"), g_axis, k)

    def stage2_onward(n, h, fr):
        g_axis = AXES[h][1]
        for k, part in ((1, "first"), (-1, "second")):
            arrived(keys["2", n, h, fr, k], ag2_ref(n, h, fr, -k, "all"))
            ag_push(("2f", n, h, fr, k), ag2_ref(n, h, fr, -k, part), g_axis, k)

    def ag_step0(n):
        for h in (0, 1):
            for k in (1, -1):
                ag_push(("1", n, h, k), ag1_ref(n, h, 0, "all"), AXES[h][0], k)
            stage2_own(n, h, 0)

    def ag_step1(n):
        for h in (0, 1):
            for k, part in ((1, "first"), (-1, "second")):
                arrived(keys["1", n, h, k], ag1_ref(n, h, -k, "all"))
                ag_push(("1f", n, h, k), ag1_ref(n, h, -k, part), AXES[h][0], k)
                stage2_own(n, h, -k)

    def ag_step2(n):
        for h in (0, 1):
            for k, part in ((1, "first"), (-1, "second")):
                arrived(keys["1f", n, h, k], ag1_ref(n, h, 2, part))
            stage2_own(n, h, 2)
            stage2_onward(n, h, 0)

    def ag_step3(n):
        for h in (0, 1):
            for fr in (-1, 1):
                stage2_onward(n, h, fr)

    def ag_step4(n):
        for h in (0, 1):
            stage2_onward(n, h, 2)

    def ag_step5(n):
        for h in (0, 1):
            for fr in (0, -1, 1, 2):
                for k, part in ((1, "first"), (-1, "second")):
                    arrived(keys["2f", n, h, fr, k], ag2_ref(n, h, fr, 2, part))

    ag_step0(0)
    loads["wd"].start()
    ag_step1(0)
    ag_step0(1)
    loaded("x")
    rotate(x_ref, 1)
    exchange(1)
    ag_step2(0)
    ag_step3(0)
    ag_step1(1)
    ag_step4(0)
    ag_step2(1)
    loaded("am", "um", "wd")

    a_own[...] = am_ref[:, :, pl.ds(pl.multiple_of(d * SLICE, SLICE), SLICE)].reshape(2 * RANK, SLICE)
    u_pad[0, :RANK] = um_ref[0]
    u_pad[1, RANK:] = um_ref[1]
    u_pad[0, RANK:] = jnp.zeros((RANK, HID), BF16)
    u_pad[1, :RANK] = jnp.zeros((RANK, HID), BF16)
    zs[...] = jnp.zeros_like(zs)
    ad_s[...] = jnp.zeros_like(ad_s)
    def adapter_down():
        tops = jnp.zeros((16, 2 * RANK), F32)
        bottoms = jnp.zeros((16, 2 * RANK), F32)
        for p in range(8):
            tokens = s_buf[1, p]
            for part in range(2):
                start = p * SLICE + part * HALF
                maps = am_ref[:, :, start : start + HALF].reshape(2 * RANK, HALF)
                value = lax.dot_general(tokens, maps, NT, preferred_element_type=F32)
                if part == 0:
                    tops = tops + value
                else:
                    bottoms = bottoms + value
        ad_s[:, : 2 * RANK] = jnp.concatenate([tops[:8] + bottoms[8:], jnp.zeros((8, 2 * RANK), F32)], axis=0).astype(BF16)

    def adapters_out():
        for k, o in rels:
            ad_keys[k, o] = send(ad_s, ad_r.at[d], (peer(k, o), t))[0]
        ad_r[d] = ad_s[...]

    def adapters_on():
        for k, o in rels:
            arrived(ad_keys[k, o], ad_r.at[source(k, o)])
        for u in range(4):
            adn[t, u] = jnp.concatenate(
                [ad_r[2 * u].astype(F32)[:8], ad_r[2 * u + 1].astype(F32)[:8]], axis=0
            ).astype(BF16)
        for i in range(1, 16):
            adt_keys[i] = send(adn.at[t], adn.at[t], (d, (t + i) % 16))[0]

    def inputs_in():
        for k, o in rels:
            arrived(first_a2a[1, k, o], r_buf.at[1, source(k, o)])
        for u in range(4):
            left, right = unpack(1, u)
            xg[u, :, :HALF] = left
            xg[u, :, HALF:] = right

    ad_keys, adt_keys, core_keys = {}, {}, {}

    def product1(i):
        rows = y_buf[i].reshape(256, SLICE)
        for start, size in TILES1:
            value = lax.dot_general(
                rows, wd[start : start + size, :], NT, preferred_element_type=F32
            ).reshape(16, 2, 8, size)
            for core in range(2):
                p_buf[i, core, :, start : start + size] = value[:, core].reshape(128, size).astype(BF16)
        core_keys[i] = send(p_buf.at[i, oc], q_buf.at[i], sib)[0]

    def add_rows(dst, others, lo=0, hi=128):
        def body(i, carry):
            value = None
            rows = pl.ds(pl.multiple_of(lo + i * 16, 16), 16)
            value = dst[0][rows, :].astype(F32)
            for ref, base in others:
                here = pl.ds(pl.multiple_of(lo - base + i * 16, 16), 16)
                value = value + ref[here, :].astype(F32)
            dst[1][rows, :] = value.astype(BF16)
            return carry

        lax.fori_loop(0, (hi - lo) // 16, body, 0)

    own = [p_buf.at[i, c] for i in range(4)]
    ag_step5(0)
    product1(0)
    ag_step0(2)
    loads["wg"].start()
    ag_step3(1)
    ag_step1(2)
    arrived(core_keys[0], q_buf.at[0])
    add_rows((own[0], own[0]), [(q_buf.at[0], 0)])
    k_f0 = send(p_buf.at[0, c, pl.ds(0, 64)], f_buf.at[0], up_dev)[0]
    k_f1 = send(p_buf.at[0, c, pl.ds(64, 64)], f_buf.at[1], down_dev)[0]
    ag_step4(1)
    ag_step2(2)
    adapter_down()
    adapters_out()
    ag_step3(2)
    loads["wu"].start()
    ag_step5(1)
    product1(1)
    ag_step4(2)
    product1(2)
    arrived(core_keys[1], q_buf.at[1])
    arrived(k_f0, f_buf.at[0])
    add_rows((own[1], own[1]), [(q_buf.at[1], 0), (f_buf.at[0], 0)], 0, 64)
    add_rows((own[1], own[1]), [(q_buf.at[1], 0)], 64, 128)
    k_g0 = send(p_buf.at[1, c], gz_buf.at[0], up_dev)[0]
    arrived(core_keys[2], q_buf.at[2])
    arrived(k_f1, f_buf.at[1])
    add_rows((own[2], own[2]), [(q_buf.at[2], 0)], 0, 64)
    add_rows((own[2], own[2]), [(q_buf.at[2], 0), (f_buf.at[1], 64)], 64, 128)
    k_g1 = send(p_buf.at[2, c], gz_buf.at[1], down_dev)[0]
    ag_step5(2)
    product1(3)
    arrived(core_keys[3], q_buf.at[3])
    add_rows((own[3], own[3]), [(q_buf.at[3], 0)])
    ab_gather.across()
    for rel in (0, 3, 1):
        ab_gather.have(rel)
        ab_gather.release(rel)
    arrived(k_g0, gz_buf.at[0])
    arrived(k_g1, gz_buf.at[1])
    add_rows((own[3], d_buf.at[z, c]), [(gz_buf.at[0], 0), (gz_buf.at[1], 0)])

    d_gather = ZGather(
        lambda u, core: d_buf.at[u, core],
        None,
    )
    d_gather.begin()
    adapters_on()
    loaded("wg", "wu")

    rs_keys = {}

    def gradients(rel):
        u = unit(rel)
        for core in range(2):

            def body(i, carry):
                rows = pl.ds(pl.multiple_of(i * 16, 16), 16)
                hidden = d_buf[u, core, rows, :].astype(F32)
                ab[u, 0, core, rows, :] = (hidden * ab[u, 0, core, rows, :].astype(F32)).astype(BF16)
                ab[u, 1, core, rows, :] = (hidden * ab[u, 1, core, rows, :].astype(F32)).astype(BF16)
                return carry

            lax.fori_loop(0, 8, body, 0)

    def by_token(value):
        pieces = []
        for i in range(16):
            pieces += [value[8 * i : 8 * i + 8], value[128 + 8 * i : 136 + 8 * i]]
        return jnp.concatenate(pieces, axis=0)

    def rank_terms(rel):
        u = unit(rel)
        gate = ab[u, 0].reshape(256, HID)
        up = ab[u, 1].reshape(256, HID)
        ranks = lax.dot_general(gate, u_pad[0], NT, preferred_element_type=F32) + lax.dot_general(
            up, u_pad[1], NT, preferred_element_type=F32
        )
        zs[:, u, :, : 2 * RANK] = by_token(ranks).astype(BF16).reshape(16, 16, 2 * RANK)
        return (SCALE * ranks).astype(BF16)

    def second(rel, ranks):
        u = unit(rel)

        def body(n, carry):
            rows = pl.ds(pl.multiple_of(n * TILE2, TILE2), TILE2)
            value = lax.dot_general(ab[u, 0].reshape(256, HID), wg[rows, :], NT, preferred_element_type=F32)
            value = value + lax.dot_general(ab[u, 1].reshape(256, HID), wu[rows, :], NT, preferred_element_type=F32)
            value = value + jnp.dot(ranks, a_own[:, rows], preferred_element_type=F32)
            o_buf[u, :, :, :, rows] = by_token(value).astype(BF16).reshape(4, 4, 16, TILE2)
            return carry

        lax.fori_loop(0, SLICE // TILE2, body, 0)

    RAXES = (("y", "x"), ("x", "y"))

    def out_block(u, h, f, g, cols):
        yy, xx = (f, g) if RAXES[h][0] == "y" else (g, f)
        return o_buf.at[u, yy, xx, :, cols]

    def add_into(dst, src):
        dst[...] = (dst[...].astype(F32) + src[...].astype(F32)).astype(BF16)

    def rs_step1(rel, h):
        u = unit(rel)
        f_axis = RAXES[h][0]
        for i, k in enumerate((1, -1)):
            rs_keys["1", rel, h, k] = send(
                out_block(u, h, shift(f_axis, 2), pl.ds(2 * i, 2), COLS[h]),
                r1.at[u, h, i],
                near(f_axis, k),
            )[0]

    def rs_step2(rel, h):
        u = unit(rel)
        f_axis = RAXES[h][0]
        for i, k in enumerate((1, -1)):
            arrived(rs_keys["1", rel, h, k], r1.at[u, h, i])
            for j in range(2):
                add_into(out_block(u, h, shift(f_axis, k), 2 * i + j, COLS[h]), r1.at[u, h, i, j])
            rs_keys["2", rel, h, k] = send(
                out_block(u, h, shift(f_axis, k), pl.ds(0, 4), COLS[h]),
                r2.at[u, h, i],
                near(f_axis, k),
            )[0]

    def rs_step3(rel, h):
        u = unit(rel)
        f_axis, g_axis = RAXES[h]
        for i, k in enumerate((1, -1)):
            arrived(rs_keys["2", rel, h, k], r2.at[u, h, i])
        for j in range(4):
            dst = out_block(u, h, pos[f_axis], j, COLS[h])
            dst[...] = (
                dst[...].astype(F32) + r2[u, h, 0, j].astype(F32) + r2[u, h, 1, j].astype(F32)
            ).astype(BF16)
        for i, k in enumerate((1, -1)):
            rs_keys["3", rel, h, k] = send(
                out_block(u, h, pos[f_axis], shift(g_axis, 2), half_cols(h, i)),
                r3.at[u, h, i],
                near(g_axis, k),
            )[0]

    def rs_step4(rel, h):
        u = unit(rel)
        f_axis, g_axis = RAXES[h]
        for i, k in enumerate((1, -1)):
            arrived(rs_keys["3", rel, h, k], r3.at[u, h, i])
            add_into(out_block(u, h, pos[f_axis], shift(g_axis, k), half_cols(h, i)), r3.at[u, h, i])
            rs_keys["4", rel, h, k] = send(
                out_block(u, h, pos[f_axis], shift(g_axis, k), COLS[h]),
                r4.at[u, h, i],
                near(g_axis, k),
            )[0]

    last_a2a = {}

    def rs_step5(rel, h):
        if h == 0:
            return
        u = unit(rel)
        halves = []
        for h in (0, 1):
            f_axis, g_axis = RAXES[h]
            for i, k in enumerate((1, -1)):
                arrived(rs_keys["4", rel, h, k], r4.at[u, h, i])
            own_block = out_block(u, h, pos[f_axis], pos[g_axis], COLS[h])[...].astype(F32)
            halves.append(own_block + r4[u, h, 0].astype(F32) + r4[u, h, 1].astype(F32))
        for core in range(2):
            rows = slice(8 * core, 8 * core + 8)
            t_buf[2 * u + core] = jnp.concatenate([halves[0][rows], halves[1][rows]], axis=0).astype(BF16)
        for o in (0, 1):
            if (rel, o) == (0, 0):
                v_buf[d] = t_buf[d]
            else:
                last_a2a[rel, o] = send(t_buf.at[peer(rel, o)], v_buf.at[d], (peer(rel, o), t))[0]

    steps = (rs_step1, rs_step2, rs_step3, rs_step4, rs_step5)

    def advance(turn):
        for k in range(5):
            if 0 <= turn - k < 4:
                for h in (0, 1):
                    steps[k](ORDER2[turn - k], h)

    def z_sum():
        for i in range(1, 16):
            arrived(z_keys[i], zr.at[(t + 16 - i) % 16])
        zr[t] = zs[t]
        total = zr[0].astype(F32)
        for i in range(1, 16):
            total = total + zr[i].astype(F32)
        turned = jnp.transpose(total.reshape(64, 128))[: 2 * RANK].astype(BF16)
        terms = jnp.dot(turned, xg[...].reshape(64, SLICE), preferred_element_type=F32)
        for i in range(16):
            ds_buf[i] = terms[:, HB * i : HB * (i + 1)].astype(BF16)
        for i in range(1, 16):
            to = (t + i) % 16
            down_keys[i] = send(ds_buf.at[to], dr_buf.at[t], (d, to))[0]
        dr_buf[t] = ds_buf[t]

    def down_sum():
        for i in range(1, 16):
            arrived(down_keys[i], dr_buf.at[(t + 16 - i) % 16])
        total = dr_buf[0].astype(F32)
        for i in range(1, 16):
            total = total + dr_buf[i].astype(F32)
        e_buf[d, t] = (total * GRAD_SCALE).astype(BF16)
        for i in range(1, 16):
            piece_keys[i] = send(e_buf.at[d, t], e_buf.at[d, t], (d, (t + i) % 16))[0]

    z_keys, down_keys, piece_keys = {}, {}, {}
    e_gather = ZGather(
        lambda u, core: e_buf.at[2 * u + core],
        lambda u, core, i: e_buf.at[2 * u + core, pl.ds(8 * i, 8)],
    )

    grads_up = [jnp.zeros((2 * RANK, HID), F32), jnp.zeros((2 * RANK, HID), F32)]

    def up_grads(rel):
        u = unit(rel)
        low = adn[:, u].astype(F32)
        rows = jnp.concatenate([low[:, :8].reshape(128, HB), low[:, 8:].reshape(128, HB)], axis=0)
        turned = jnp.transpose(rows)[: 2 * RANK].astype(BF16)
        for i in range(2):
            grads_up[i] = grads_up[i] + jnp.dot(turned, ab[u, i].reshape(256, HID), preferred_element_type=F32)

    d_gather.have(0)
    gradients(0)
    second(0, rank_terms(0))
    advance(0)
    inputs_in()
    d_gather.across()
    d_gather.have(3)
    gradients(3)
    ab_gather.pass_up()
    d_gather.have(1)
    gradients(1)
    ab_gather.pass_down()
    second(3, rank_terms(3))
    advance(1)
    second(1, rank_terms(1))
    ab_gather.last()
    advance(2)
    ab_gather.have(2)
    ranks = rank_terms(2)
    for i in range(1, 16):
        to = (t + i) % 16
        z_keys[i] = send(zs.at[to], zr.at[t], (d, to))[0]
    second(2, ranks)
    advance(3)
    z_sum()
    advance(4)
    down_sum()
    advance(5)
    for i in range(1, 16):
        arrived(piece_keys[i], e_buf.at[d, (t + 16 - i) % 16])
    e_gather.begin()
    advance(6)
    for i in range(1, 16):
        arrived(adt_keys[i], adn.at[(t + 16 - i) % 16])
    for rel in range(4):
        up_grads(rel)
    up_ref[0] = grads_up[0][:RANK] * GRAD_SCALE
    up_ref[1] = grads_up[1][RANK:] * GRAD_SCALE
    stores = [pltpu.make_async_copy(up_ref, up_hbm, ws.at[0])]
    stores[0].start()
    e_gather.across()
    e_gather.pass_up()
    e_gather.pass_down()
    advance(7)
    e_gather.last()
    for rel in range(4):
        e_gather.have(rel)
    stores.append(pltpu.make_async_copy(e_buf, e_hbm, ws.at[1]))
    stores[1].start()
    for k, o in rels:
        arrived(last_a2a[k, o], v_buf.at[source(k, o)])
    stores.append(pltpu.make_async_copy(v_buf, v_hbm, ws.at[2]))
    stores[2].start()
    for copy in pending:
        copy.wait_send()
    for copy in stores:
        copy.wait()
    assert count[0] == NSEM


def finish(v_ref, e_ref, up_in, out_ref, down_ref, up_ref):
    for p in range(8):
        value = v_ref[p]
        out_ref[0, :, p * SLICE : p * SLICE + HALF] = value[:8]
        out_ref[0, :, p * SLICE + HALF : (p + 1) * SLICE] = value[8:]
        for i in range(16):
            start = p * SLICE + HB * i
            down_ref[:, start : start + HB] = e_ref[p, i].astype(F32)
    up_ref[...] = up_in[...]


def on_device(kept, grad, gate_pre, up_pre, wg, wu, wd, a_maps, u_maps):
    vmem = pl.BlockSpec(memory_space=pltpu.VMEM)
    hbm = pl.BlockSpec(memory_space=pl.ANY)
    operands = [
        (1, 8, WIDTH), (1, 8, WIDTH), (1, 128, HID), (1, 128, HID), (2, RANK, WIDTH), (2, RANK, HID), (HB, HB),
    ]
    shapes = [
        (HID, SLICE), (SLICE, HID), (SLICE, HID),
        (2, 8, 16, HALF), (2, 8, 16, HALF),
        (4, 4, 4, 16, SLICE),
        (4, 16, SLICE),
        (4, 2, 128, HID), (4, 128, HID), (2, 64, HID), (2, 128, HID), (4, 2, 128, HID),
        (4, 2, 2, 128, HID),
        (4, 4, 4, 16, SLICE),
        (4, 2, 2, 2, 16, HALF), (4, 2, 2, 4, 16, HALF), (4, 2, 2, 16, 512), (4, 2, 2, 16, HALF),
        (8, 16, HALF), (8, 16, HALF),
        (16, HB), (8, 16, HB), (16, 4, 16, HB),
        (16, 4, 16, HB), (16, 4, 16, HB),
        (16, 2 * RANK, HB), (16, 2 * RANK, HB), (8, 16, 2 * RANK, HB),
        (2 * RANK, SLICE), (2, 2 * RANK, HID),
    ]
    results = pl.pallas_call(
        kernel,
        out_shape=(
            jax.ShapeDtypeStruct((8, 16, HALF), BF16),
            jax.ShapeDtypeStruct((8, 16, 2 * RANK, HB), BF16),
            jax.ShapeDtypeStruct((2, RANK, HID), F32),
        ),
        in_specs=[hbm] * 10,
        out_specs=(hbm,) * 3,
        scratch_shapes=[pltpu.VMEM(s, BF16) for s in operands]
        + [pltpu.VMEM((2, RANK, HID), F32)]
        + [pltpu.VMEM(s, BF16) for s in shapes]
        + [
            pltpu.SemaphoreType.DMA((NSEM,)),
            pltpu.SemaphoreType.DMA((NSEM,)),
            pltpu.SemaphoreType.DMA((10,)),
        ],
        compiler_params=pltpu.CompilerParams(
            collective_id=0, has_side_effects=True, vmem_limit_bytes=66_000_000
        ),
        name="gated_backward",
    )(kept, grad, gate_pre, up_pre, a_maps, u_maps, jnp.asarray(sign_table(), BF16), wd, wg, wu)
    out, down, up = pl.pallas_call(
        finish,
        out_shape=(
            jax.ShapeDtypeStruct((1, 8, WIDTH), BF16),
            jax.ShapeDtypeStruct((2 * RANK, WIDTH), F32),
            jax.ShapeDtypeStruct((2, RANK, HID), F32),
        ),
        in_specs=[vmem] * 3,
        out_specs=(vmem,) * 3,
        name="finish",
    )(*results)
    return out, down.reshape(2, RANK, WIDTH), up


def solution(mesh):
    placed = (
        P("dp", "tensor", None),
        P("dp", "tensor", None),
        P("dp", None, "tensor"),
        P("dp", None, "tensor"),
        P("dp", "tensor"),
        P("dp", "tensor"),
        P("tensor", "dp"),
        P(),
        P(None, None, "tensor"),
    )
    return jax.shard_map(
        on_device,
        mesh=mesh,
        in_specs=placed,
        out_specs=(P("dp", "tensor", None), P(), P(None, None, "tensor")),
        check_vma=False,
    )
```
